256 devices in a mesh: section: 16 (over y, x_lo, core), tensor: 16 (over x_hi, z).
Axes of the slice: x: 4 (x_hi: 2, x_lo: 2; x = x_hi * 2 + x_lo), y: 4, z: 8, core: 2. Of those that a mesh axis runs over, the one named last changes fastest.
Arguments:
- states: bfloat16 [8192, 8192], P('section', 'tensor'), may hold values from -6 to 6
- lengths: int32 [16, 16], P('section'), may hold values from 1 to 96, 512 in all within a row
- routes: int32 [8192, 1], P('section'), may hold values from 0 to 15; in each aligned block of 512 rows (0 to 511, 512 to 1023, ...) at most 64 rows name the same one
- score_gain: float32 [16, 8192], P('section'), may hold values from 0.25 to 1.75
- score_weight: bfloat16 [16, 8192, 4096], P('section', None, 'tensor'), may hold values from -0.0625 to 0.0625
- score_heads: float32 [16, 4096, 2], P('section', 'tensor'), may hold values from -0.09375 to 0.09375
- actor_gain: float32 [8192], replicated, may hold values from 0.25 to 1.75
- actor_weight: bfloat16 [8192, 4096], P(None, 'tensor'), may hold values from -0.0625 to 0.0625
- actor_heads: float32 [4096], P('tensor'), may hold values from -0.09375 to 0.09375
Outputs:
- packed_scores: float32 [2, 16384], P(None, 'section')
- advantages: float32 [8192], P('section')
- actor_grad: float32 [8192, 4096], P('section', 'tensor')
The draws below stay inside these ranges and needn't reach their ends.
Inputs may be any that keep to these rules, and one draw needn't show every extreme that they name: `lengths`: each row sums to 512; its largest entry is exactly 96. `routes`: in the rows of one section (aligned blocks of 512 rows) no member is named by more than 64 rows; some member is named by exactly 64 rows of some block.
All inputs are finite; a program needn't handle non-finite values.
Results may differ from the reference program's by a relative error of at most 0.0055.
Values may be sent and summed in bfloat16 or wider, within the bound.
No kernel may reach another device: no remote copies, remote signals or barrier semaphores. Data moves between devices by JAX's collectives and lax.ppermute only.
A program may use at most 128 MiB of HBM per device.

```python
import math
import jax
import jax.numpy as jnp
import numpy as np
from jax import lax

D = 8192
HID = 4096
TOK_SEC = 512
RESP_SEC = 16
LEN_MAX = 96
CAP = 64
SLOTS = 1024
TOKENS = 8192
N_SECTION = 16


def level_of(key, extent, shards, low, top_value):
    gain = 1.0
    for dim, parts in shards:
        steps = jax.random.uniform(jax.random.fold_in(jax.random.fold_in(key, 6), dim), (parts,), jnp.float32, low / len(shards), top_value / len(shards))
        gain = gain * jnp.repeat(jnp.exp(steps), extent[dim] // parts).reshape((-1,) + (1,) * (len(extent) - 1 - dim))
    return gain


def split_up(amount, total, bound, lean):
    loads = [(1 << 20) // math.isqrt(standing ** lean) + 1 for standing in range(2, amount + 1)]
    rest, holding = total - bound - (amount - 1), [1] * (amount - 1)
    while rest > 0:
        candidates = [i for i in range(amount - 1) if holding[i] < bound]
        mass, budget = sum([loads[i] for i in candidates]), rest
        for i in candidates:
            extra = min(bound - holding[i], max(1, budget * loads[i] // mass), rest)
            holding[i] = holding[i] + extra
            rest = rest - extra
    return np.array([bound] + holding)


def uneven(stream_key, count, total, limit, skew):
    if count == 2:
        one = jax.random.randint(stream_key, (), max(1, total - limit), min(limit, total - 1) + 1)
        return jnp.stack([one, total - one])
    tallies = jnp.asarray(split_up(count, total, limit, skew), jnp.int32)
    couples = (count - 1) // 2
    giver, receiver = tallies[1:1 + 2 * couples:2], tallies[2:2 + 2 * couples:2]
    margin = jnp.minimum(giver - 1, limit - receiver)
    passed = jax.random.randint(jax.random.fold_in(stream_key, 1), (couples,), 0, 1 << 20) % (margin + 1)
    tallies = tallies.at[1:1 + 2 * couples:2].set(giver - passed).at[2:2 + 2 * couples:2].set(receiver + passed)
    return tallies[jax.random.permutation(jax.random.fold_in(stream_key, 2), count)]


def shared_out(stream_key, own, number, rows, count, top, limit, lean):
    order = jax.random.permutation(stream_key, count)
    crowded, common = shares(count, rows * top, limit, lean, True), shares(count, rows * top, limit, lean, False)
    places = jnp.arange(count)

    def named(sizes, rotation):
        used = int((sizes > 0).sum())
        fixed = max(1, used // 4)
        shifted = fixed + (places - fixed + rotation * (used - fixed)) % max(1, count - fixed)
        return jnp.zeros((count,), jnp.int32).at[order[jnp.where(places < fixed, places, shifted)]].set(jnp.asarray(sizes, jnp.int32))

    sizes = jnp.where(number % 4 == 0, named(crowded, number // 4), named(common, number - number // 4 - 1))
    mixed = jax.random.permutation(jax.random.fold_in(own, 3), count)
    giver, receiver = mixed[0:count // 2 * 2:2], mixed[1:count // 2 * 2:2]
    margin = jnp.minimum(sizes[giver] - 1, limit - sizes[receiver]) // 2
    margin = jnp.where((giver == order[0]) | (receiver == order[0]) | (sizes[receiver] == 0), 0, jnp.maximum(margin, 0))
    shifted = jax.random.randint(jax.random.fold_in(own, 4), (count // 2,), 0, 1 << 20) % (margin + 1)
    sizes = sizes.at[giver].add(-shifted).at[receiver].add(shifted)
    labels = jnp.searchsorted(jnp.cumsum(sizes), jnp.arange(rows * top), side="right").astype(jnp.int32)
    grid = labels.reshape(top, rows).T
    grid = grid[jax.random.permutation(jax.random.fold_in(own, 1), rows)]
    rotation = jax.random.randint(jax.random.fold_in(own, 2), (rows, 1), 0, top)
    return jnp.take_along_axis(grid, (jnp.arange(top)[None, :] + rotation) % top, axis=1)


def shares(count, total, limit, slope, full):
    loads = [(1 << 20) // math.isqrt(standing ** slope) + 1 for standing in range(1, count + 1)]
    largest = limit if full else min(limit, max(-(-total // count), total * loads[0] // sum(loads)))
    least = 1 if total - largest >= count - 1 else 0
    counts, spare = [largest] + [least] * (count - 1), total - largest - least * (count - 1)
    while spare > 0:
        candidates = [i for i in range(1, count) if counts[i] < largest] or [i for i in range(1, count) if counts[i] < limit]
        mass, budget = sum([loads[i] for i in candidates]), spare
        for i in candidates:
            extra = min(limit - counts[i], max(1, budget * loads[i] // mass), spare)
            counts[i] = counts[i] + extra
            spare = spare - extra
    return np.array(counts)


def normal_values(rng, shape, scale, limit, pieces=(), held_as=jnp.bfloat16):
    array = scale * jax.random.normal(rng, shape, jnp.float32)
    if pieces:
        array = array * level_of(rng, shape, pieces, -0.22, 0.18)
    return jnp.clip(array, -limit, limit).astype(held_as)


def setup_inputs(seed: int = 0) -> dict:
    splits = jax.random.split(jax.random.key(seed), 10)
    states = normal_values(splits[0], (TOKENS, D), 1.0, 6.0, ((0, 16), (1, 16)))
    lengths = jax.vmap(lambda own: uneven(own, RESP_SEC, TOK_SEC, LEN_MAX, 2))(jax.random.split(splits[1], N_SECTION)).reshape((N_SECTION, RESP_SEC)).astype(jnp.int32)
    routes_keys = jax.random.split(jax.random.fold_in(splits[2], 1), TOKENS // TOK_SEC)
    routes_turns = jax.random.permutation(jax.random.fold_in(splits[2], 3), TOKENS // TOK_SEC)
    routes = jax.vmap(lambda own, number: shared_out(jax.random.fold_in(splits[2], 2), own, number, TOK_SEC, N_SECTION, 1, CAP, 2))(routes_keys, routes_turns).reshape((TOKENS, 1))
    score_gain = jnp.clip(1.0 + 0.15 * jax.random.normal(splits[3], (N_SECTION, D), jnp.float32), 0.25, 1.75)
    score_weight = normal_values(splits[4], (N_SECTION, D, HID), D ** -0.5, 0.0625, ((0, 16), (2, 16)))
    score_heads = normal_values(splits[5], (N_SECTION, HID, 2), HID ** -0.5, 0.09375, ((0, 16), (1, 16)), jnp.float32)
    actor_gain = jnp.clip(1.0 + 0.15 * jax.random.normal(splits[6], (D,), jnp.float32), 0.25, 1.75)
    actor_weight = normal_values(splits[7], (D, HID), D ** -0.5, 0.0625, ((1, 16),))
    actor_heads = normal_values(splits[8], (HID,), HID ** -0.5, 0.09375, ((0, 16),), jnp.float32)
    return {"states": states, "lengths": lengths, "routes": routes, "score_gain": score_gain, "score_weight": score_weight, "score_heads": score_heads, "actor_gain": actor_gain, "actor_weight": actor_weight, "actor_heads": actor_heads}


epsilon = 1e-05
trace_decay = 0.95
penalty = 0.1

def compose(earlier, later):
    return (earlier[0] * later[0], later[1] + later[0] * earlier[1])

def advantage_rows(values, rewards, lengths):
    ends = jnp.cumsum(lengths, axis=1) - 1
    steps_idx = jnp.arange(values.shape[1], dtype=jnp.int32)
    last = jnp.any(steps_idx[None, :, None] == ends[:, None, :], axis=2)
    following = jnp.concatenate([values[:, 1:], jnp.zeros_like(values[:, :1])], axis=1)
    delta = jnp.where(last, rewards, following) - values
    weight = jnp.where(last, 0.0, trace_decay).astype(values.dtype)
    carried = lax.associative_scan(compose, (weight[:, ::-1], delta[:, ::-1]), axis=1)
    return carried[1][:, ::-1]

def reference(states, lengths, routes, score_gain, score_weight, score_heads, actor_gain, actor_weight, actor_heads):
    target = routes[:, 0].astype(jnp.int32)
    source = (jnp.arange(TOKENS, dtype=jnp.int32) // TOK_SEC).astype(jnp.int32)
    onehot = (target[:, None] == jnp.arange(N_SECTION, dtype=jnp.int32)[None, :]).astype(jnp.int32)
    blocked = onehot.reshape(N_SECTION, TOK_SEC, N_SECTION)
    before = (jnp.cumsum(blocked, axis=1) - blocked).reshape(TOKENS, N_SECTION)
    placed = lax.optimization_barrier(jnp.sum(before * onehot, axis=1)).astype(jnp.int32)
    slot_index = (source * CAP + placed).astype(jnp.int32)
    packed = jnp.zeros((N_SECTION, SLOTS, D), jnp.bfloat16).at[target, slot_index].set(states)

    def member(member_args):
        row_block, gain_row, member_weight, head_cols = member_args
        widened = row_block.astype(jnp.float32)
        member_scale = lax.rsqrt(lax.optimization_barrier(jnp.mean(widened * widened, axis=1)) + epsilon)
        scaled = (widened * gain_row[None, :]).astype(jnp.bfloat16)
        preact = jnp.dot(scaled, member_weight, preferred_element_type=jnp.float32) * member_scale[:, None]
        return jnp.dot(jax.nn.silu(preact), head_cols, precision=lax.Precision.HIGHEST)
    scored = lax.map(member, (packed, score_gain, score_weight, score_heads))
    packed_scores = jnp.transpose(scored, (2, 0, 1)).reshape(2, N_SECTION * SLOTS)
    token_scores = scored[target, slot_index]
    values = token_scores[:, 0].reshape(N_SECTION, TOK_SEC)
    rewards = token_scores[:, 1].reshape(N_SECTION, TOK_SEC)
    raw_adv = advantage_rows(values, rewards, lengths)
    center = jnp.sum(raw_adv) / TOKENS
    spread = jnp.sum(raw_adv * raw_adv) / TOKENS - center * center
    advantages = ((raw_adv - center) * lax.rsqrt(spread + epsilon)).reshape(TOKENS)
    widened = states.astype(jnp.float32)
    actor_scale = lax.rsqrt(lax.optimization_barrier(jnp.mean(widened * widened, axis=1)) + epsilon)
    gained = (widened * actor_gain[None, :]).astype(jnp.bfloat16)
    actor_pre = jnp.dot(gained, actor_weight, preferred_element_type=jnp.float32) * actor_scale[:, None]
    log_shift = jnp.dot(jax.nn.silu(actor_pre), actor_heads, precision=lax.Precision.HIGHEST)
    ratios = jnp.exp(log_shift)
    logit_slope = penalty * (ratios - 1.0) - ratios * advantages
    sigmoid_pre = jax.nn.sigmoid(actor_pre)
    silu_slope = sigmoid_pre * (1.0 + actor_pre * (1.0 - sigmoid_pre))
    grad_pre = ((logit_slope * actor_scale)[:, None] * actor_heads[None, :] * silu_slope).astype(jnp.bfloat16)
    actor_grad = jnp.dot(gained.T, grad_pre, preferred_element_type=jnp.float32)
    return (packed_scores, advantages, actor_grad)
```

```python
import jax
import jax.numpy as jnp
from jax import lax
from jax.sharding import Mesh, PartitionSpec as P

epsilon = 1e-05
trace_decay = 0.95
penalty = 0.1

SECTION = ("y", "l", "c")
MEMBER = ("y", "l", "h")
SLICE = ("c", "z")


def flip(v):
    return lax.ppermute(v, ("c", "h"), [(0, 0), (1, 2), (2, 1), (3, 3)])


def flip_near(v):
    pairs = []
    for l in range(2):
        for c in range(2):
            for h in range(2):
                to = (l, c, h) if c == h else (1 - l, h, c)
                pairs.append((l * 4 + c * 2 + h, to[0] * 4 + to[1] * 2 + to[2]))
    return lax.ppermute(v, ("l", "c", "h"), pairs)


def spread(v, axes):
    return lax.all_to_all(
        jnp.broadcast_to(v[None], (16,) + v.shape), axes, split_axis=0, concat_axis=0, tiled=True
    )


def number(axes):
    return lax.axis_index(axes)


def shifted(v, k):
    return jnp.concatenate([v[:, k:], jnp.zeros_like(v[:, :k])], axis=1)


def body(
    states,
    lengths,
    routes,
    score_gain,
    score_weight,
    score_heads,
    actor_gain,
    actor_weight,
    actor_heads,
):
    toks = states.shape[0]
    feats = states.shape[1]
    width = actor_gain.shape[0]
    hid = actor_heads.shape[0]
    parts = 16
    cap = 2 * toks // parts
    slots = parts * cap
    half = slots // 2
    ring = 8
    me_z = number("z")
    me_c = number("c")
    section = number(SECTION)
    member = number(MEMBER)

    meta = flip(jnp.concatenate([routes[:, 0], lengths[0]]))
    moved = flip(states)
    target = meta[:toks]
    spans = meta[toks:]

    heads = flip(jnp.concatenate([score_heads[0].T, actor_heads[None]], axis=0))
    score_w = flip((score_weight[0] * score_gain[0][:, None]).astype(jnp.bfloat16))
    actor_w = flip_near((actor_weight * actor_gain[:, None]).astype(jnp.bfloat16))

    pos = jnp.arange(toks, dtype=jnp.int32)
    onehot = target[:, None] == jnp.arange(parts, dtype=jnp.int32)[None, :]
    earlier = (pos[:, None] > pos[None, :]).astype(jnp.bfloat16)
    before = jnp.dot(earlier, onehot.astype(jnp.bfloat16), preferred_element_type=jnp.float32)
    placed = jnp.sum(jnp.where(onehot, before, 0.0), axis=1).astype(jnp.int32)
    slot = target * cap + placed
    order = jnp.arange(spans.shape[0], dtype=jnp.int32)
    ends = jnp.sum(jnp.where(order[:, None] >= order[None, :], spans[None, :], 0), axis=1) - 1
    last = jnp.any(pos[:, None] == ends[None, :], axis=1)
    codes = lax.all_gather(slot * 2 + last.astype(jnp.int32), MEMBER)

    dispatch = (jnp.arange(slots, dtype=jnp.int32)[:, None] == slot[None, :]).astype(jnp.bfloat16)
    outbox = jnp.dot(dispatch, moved, preferred_element_type=jnp.float32).astype(jnp.bfloat16)
    packed = lax.all_to_all(
        outbox.reshape(parts, cap, feats), MEMBER, split_axis=0, concat_axis=0, tiled=True
    ).reshape(slots, feats)

    wide = packed.astype(jnp.float32)
    squares = jnp.sum(
        lax.all_gather(jnp.sum(wide * wide, axis=1).reshape(8, slots // 8), SLICE), axis=0
    ).reshape(slots)
    scale = lax.rsqrt(squares / width + epsilon)

    right = [(i, (i + 1) % ring) for i in range(ring)]
    left = [(i, (i - 1) % ring) for i in range(ring)]
    other = [(0, 1), (1, 0)]
    score_b = score_w.reshape(parts, feats, hid)
    actor_b = actor_w.reshape(parts, feats, hid)

    def add(total, block, core, where):
        index = core * ring + where
        terms = [
            jnp.dot(
                block,
                lax.dynamic_index_in_dim(w, index, 0, keepdims=False),
                preferred_element_type=jnp.float32,
            )
            for w in (score_b, actor_b)
        ]
        return terms if total is None else [t + a for t, a in zip(total, terms)]

    top, low = packed[:half], packed[half:]
    tops, lows, tops_o, lows_o = [], [], [], []
    sum_t = sum_l = None
    for i in range(ring):
        tops.append(top)
        lows.append(low)
        top_o = lax.ppermute(top, "c", other)
        low_o = lax.ppermute(low, "c", other)
        tops_o.append(top_o)
        lows_o.append(low_o)
        if i < ring - 1:
            top = lax.ppermute(top, "z", right)
            low = lax.ppermute(low, "z", left)
        back, ahead = (me_z - i) % ring, (me_z + i) % ring
        sum_t = add(sum_t, tops[i], me_c, back)
        sum_l = add(sum_l, lows[i], me_c, ahead)
        sum_t = add(sum_t, top_o, 1 - me_c, back)
        sum_l = add(sum_l, low_o, 1 - me_c, ahead)
    score_pre = jnp.concatenate([sum_t[0], sum_l[0]], axis=0) * scale[:, None]
    actor_pre = jnp.concatenate([sum_t[1], sum_l[1]], axis=0) * scale[:, None]
    part_score = lax.dot_general(
        heads[:2], jax.nn.silu(score_pre), (((1,), (1,)), ((), ())), precision=lax.Precision.HIGHEST
    )
    part_shift = lax.dot_general(
        heads[2:], jax.nn.silu(actor_pre), (((1,), (1,)), ((), ())), precision=lax.Precision.HIGHEST
    )
    totals = jnp.sum(spread(jnp.concatenate([part_score, part_shift], axis=0), SLICE), axis=0)
    scores = spread(totals[:2], MEMBER)
    packed_scores = lax.dynamic_index_in_dim(scores, section, 0, keepdims=False)

    every_slot = codes // 2
    every_target = every_slot // cap
    every_place = every_slot % cap
    final = (codes % 2) == 1
    at_place = (every_place[:, :, None] == jnp.arange(cap, dtype=jnp.int32)).astype(jnp.float32)
    at_target = (every_target[:, :, None] == jnp.arange(parts, dtype=jnp.int32)).astype(jnp.float32)
    table = scores.reshape(parts, 2, parts, cap)
    found = jnp.einsum("stj,mksj->kstm", at_place, table, precision=lax.Precision.HIGHEST)
    found = jnp.sum(found * at_target[None], axis=3)
    values, rewards = found[0], found[1]
    raw = jnp.where(final, rewards, shifted(values, 1)) - values
    weight = jnp.where(final, 0.0, trace_decay)
    step = 1
    while step < 128:
        raw = raw + weight * shifted(raw, step)
        weight = weight * shifted(weight, step)
        step *= 2
    total_tokens = raw.size
    center = jnp.sum(raw) / total_tokens
    spread_sq = jnp.sum(raw * raw) / total_tokens - center * center
    every_adv = (raw - center) * lax.rsqrt(spread_sq + epsilon)
    advantages = lax.dynamic_index_in_dim(every_adv, section, 0, keepdims=False)
    mine = jnp.where(every_target == member, every_adv, 0.0)
    adv_slot = jnp.sum(mine[:, :, None] * at_place, axis=1).reshape(slots)

    ratios = jnp.exp(totals[2])
    slope = penalty * (ratios - 1.0) - ratios * adv_slot
    sig = jax.nn.sigmoid(actor_pre)
    silu_slope = sig * (1.0 + actor_pre * (1.0 - sig))
    grad_pre = ((slope * scale)[:, None] * heads[2][None, :] * silu_slope).astype(jnp.bfloat16)

    terms = jnp.zeros((parts, hid, feats), jnp.bfloat16)
    for core, ts, ls in ((me_c, tops, lows), (1 - me_c, tops_o, lows_o)):
        for i in range(ring):
            block = jnp.concatenate([ts[i], ls[(ring - i) % ring]], axis=0)
            term = lax.dot_general(
                grad_pre, block, (((0,), (0,)), ((), ())), preferred_element_type=jnp.float32
            )
            terms = lax.dynamic_update_index_in_dim(
                terms, term.astype(jnp.bfloat16), core * ring + (me_z - i) % ring, 0
            )
    arrived = lax.all_to_all(terms, MEMBER, split_axis=0, concat_axis=0, tiled=True)
    grad = flip(jnp.sum(arrived.astype(jnp.float32), axis=0))
    gain = lax.dynamic_slice_in_dim(actor_gain, section * feats, feats)
    actor_grad = grad.T * gain[:, None]
    return (packed_scores, advantages, actor_grad)


def solution(mesh):
    fine = Mesh(mesh.devices.reshape(4, 2, 2, 2, 8), ("y", "l", "c", "h", "z"))
    tensor = ("h", "z")
    in_specs = (
        P(SECTION, tensor),
        P(SECTION, None),
        P(SECTION, None),
        P(SECTION, None),
        P(SECTION, None, tensor),
        P(SECTION, tensor, None),
        P(),
        P(None, tensor),
        P(tensor),
    )
    out_specs = (P(None, SECTION), P(SECTION), P(SECTION, tensor))
    return jax.shard_map(body, mesh=fine, in_specs=in_specs, out_specs=out_specs, check_vma=False)
```

```python
import jax
import jax.numpy as jnp
from jax import lax
from jax.experimental import pallas as pl
from jax.experimental.pallas import tpu as pltpu
from jax.sharding import Mesh, PartitionSpec as P

epsilon = 1e-05
trace_decay = 0.95
penalty = 0.1

SECTION = ("y", "l", "c")
MEMBER = ("y", "l", "h")
SLICE = ("c", "z")


def at_home():
    return lax.axis_index("c") == lax.axis_index("h")


def flip(v):
    got = lax.ppermute(v, ("c", "h"), [(1, 2), (2, 1)])
    return jnp.where(at_home(), v, got)


def flip_far(v):
    return lax.ppermute(v, ("c", "h"), [(1, 2), (2, 1)])


def flip_near(v):
    pairs = [(l * 4 + a, (1 - l) * 4 + b) for l in range(2) for a, b in ((1, 2), (2, 1))]
    got = lax.ppermute(v, ("l", "c", "h"), pairs)
    return jnp.where(at_home(), v, got)


def gather_steps(place, blocks, weight, gain, total, with_squares):
    rows, feats = blocks[0].shape
    hid = weight.shape[2]
    cols = hid + (128 if with_squares else 0)
    tile = rows // 2
    count = len(blocks)

    def kernel(place_ref, *refs):
        xs, ws, gs = refs[:count], refs[count : 2 * count], refs[2 * count : 3 * count]
        out_ref = refs[-1]
        for side in range(2):
            acc = None if total is None else refs[3 * count][side, :, :hid]
            squares = None
            if with_squares:
                squares = (
                    jnp.zeros((tile, 128), jnp.float32)
                    if total is None
                    else refs[3 * count][side, :, hid:]
                )
            for k in range(count):
                if k % 4 // 2 != side:
                    continue
                wide = xs[k][...].astype(jnp.float32)
                scaled = (wide * gs[k][0]).astype(jnp.bfloat16)
                term = jnp.dot(scaled, ws[k][0], preferred_element_type=jnp.float32)
                acc = term if acc is None else acc + term
                if with_squares:
                    square = wide * wide
                    for j in range(feats // 128):
                        squares = squares + square[:, j * 128 : (j + 1) * 128]
            out_ref[side, :, :hid] = acc
            if with_squares:
                out_ref[side, :, hid:] = squares

    def pick(shape, at):
        return pl.BlockSpec(shape, lambda r, p: (p[at], 0, 0))

    x_spec = pl.BlockSpec((tile, feats), lambda r, p: (r, 0))
    acc_spec = pl.BlockSpec((2, tile, cols), lambda r, p: (0, r, 0))
    in_specs = [x_spec] * count
    in_specs += [pick((1, feats, hid), at) for at in range(count)]
    in_specs += [pick((1, 1, feats), count + at) for at in range(count)]
    operands = [place, *blocks] + [weight] * count + [gain] * count
    aliases = {}
    if total is not None:
        aliases = {len(operands): 0}
        operands.append(total)
        in_specs.append(acc_spec)
    return pl.pallas_call(
        kernel,
        out_shape=jax.ShapeDtypeStruct((2, rows, cols), jnp.float32),
        grid_spec=pltpu.PrefetchScalarGridSpec(
            num_scalar_prefetch=1, grid=(2,), in_specs=in_specs, out_specs=acc_spec
        ),
        input_output_aliases=aliases,
        compiler_params=pltpu.CompilerParams(vmem_limit_bytes=60 << 20),
        cost_estimate=pl.CostEstimate(
            flops=2 * count * rows * feats * hid,
            bytes_accessed=(3 * count // 2 + 5) << 19,
            transcendentals=0,
        ),
    )(*operands)


def gradient_terms(place, slope_t, halves):
    count = len(halves) // 2
    hid = slope_t.shape[0]
    rows, feats = halves[0].shape

    def kernel(place_ref, slope_ref, *refs):
        blocks = refs[: 2 * count]
        out_ref, held, made, sems, out_sems = refs[2 * count :]

        def fetch(k, side):
            return pltpu.make_async_copy(
                blocks[2 * k + side], held.at[k, pl.ds(side * rows, rows)], sems.at[k, side]
            )

        def put(k):
            return pltpu.make_async_copy(made.at[k], out_ref.at[place_ref[k]], out_sems.at[k])

        for k in range(count):
            for side in range(2):
                fetch(k, side).start()
        for k in range(count):
            for side in range(2):
                fetch(k, side).wait()
            made[k] = jnp.dot(
                slope_ref[...], held[k], preferred_element_type=jnp.float32
            ).astype(jnp.bfloat16)
            put(k).start()
        for k in range(count):
            put(k).wait()

    anywhere = pl.BlockSpec(memory_space=pl.ANY)
    return pl.pallas_call(
        kernel,
        out_shape=jax.ShapeDtypeStruct((count, hid, feats), jnp.bfloat16),
        grid_spec=pltpu.PrefetchScalarGridSpec(
            num_scalar_prefetch=1,
            grid=(1,),
            in_specs=[pl.BlockSpec((hid, 2 * rows), lambda r, p: (0, 0))] + [anywhere] * (2 * count),
            out_specs=anywhere,
            scratch_shapes=[
                pltpu.VMEM((count, 2 * rows, feats), jnp.bfloat16),
                pltpu.VMEM((count, hid, feats), jnp.bfloat16),
                pltpu.SemaphoreType.DMA((count, 2)),
                pltpu.SemaphoreType.DMA((count,)),
            ],
        ),
        compiler_params=pltpu.CompilerParams(vmem_limit_bytes=60 << 20),
        cost_estimate=pl.CostEstimate(
            flops=2 * count * 2 * rows * feats * hid, bytes_accessed=21 << 20, transcendentals=0
        ),
    )(place, slope_t, *halves)


def spread(v, axes):
    return lax.all_to_all(
        jnp.broadcast_to(v[None], (16,) + v.shape), axes, split_axis=0, concat_axis=0, tiled=True
    )


def number(axes):
    return lax.axis_index(axes)


def shifted(v, k):
    return jnp.concatenate([v[:, k:], jnp.zeros_like(v[:, :k])], axis=1)


def body(
    states,
    lengths,
    routes,
    score_gain,
    score_weight,
    score_heads,
    actor_gain,
    actor_weight,
    actor_heads,
):
    toks = states.shape[0]
    feats = states.shape[1]
    width = actor_gain.shape[0]
    hid = actor_heads.shape[0]
    parts = 16
    cap = 2 * toks // parts
    slots = parts * cap
    half = slots // 2
    ring = 8
    me_z = number("z")
    me_c = number("c")
    section = number(SECTION)
    member = number(MEMBER)

    meta = flip(jnp.concatenate([routes[:, 0], lengths[0]]))
    moved = flip(states)
    target = meta[:toks]
    spans = meta[toks:]
    pos = jnp.arange(toks, dtype=jnp.int32)
    onehot = target[:, None] == jnp.arange(parts, dtype=jnp.int32)[None, :]
    earlier = (pos[:, None] > pos[None, :]).astype(jnp.bfloat16)
    before = jnp.dot(earlier, onehot.astype(jnp.bfloat16), preferred_element_type=jnp.float32)
    placed = jnp.sum(jnp.where(onehot, before, 0.0), axis=1).astype(jnp.int32)
    slot = target * cap + placed
    order = jnp.arange(spans.shape[0], dtype=jnp.int32)
    ends = jnp.sum(jnp.where(order[:, None] >= order[None, :], spans[None, :], 0), axis=1) - 1
    last = jnp.any(pos[:, None] == ends[None, :], axis=1)
    code = (slot * 2 + last.astype(jnp.int32)).astype(jnp.float32)

    (near_w, own_heads, own_shift, own_gain), meta = lax.optimization_barrier(
        ((actor_weight, score_heads, actor_heads, score_gain), meta)
    )
    small = flip(
        jnp.concatenate([own_heads[0].T.reshape(-1), own_shift, own_gain[0]], axis=0)
    )
    me_y = number("y")
    share = width // 4
    quarter = flip_near(lax.dynamic_slice_in_dim(near_w, me_y * share, share))

    dispatch = (jnp.arange(slots, dtype=jnp.int32)[:, None] == slot[None, :]).astype(jnp.bfloat16)
    outbox = jnp.dot(dispatch, moved, preferred_element_type=jnp.float32).astype(jnp.bfloat16)
    packed = lax.all_to_all(
        outbox.reshape(parts, cap, feats), MEMBER, split_axis=0, concat_axis=0, tiled=True
    ).reshape(slots, feats)

    (late_w, small, quarter), packed = lax.optimization_barrier(
        ((score_weight[0], small, quarter), packed)
    )
    score_b = flip_far(late_w)
    heads = small[: 3 * hid].reshape(3, hid)
    gains = (small[3 * hid :].reshape(parts, 1, feats), actor_gain.reshape(parts, 1, feats))
    quarters = [quarter] + [
        lax.ppermute(quarter, "y", [(i, (i + d) % 4) for i in range(4)]) for d in (1, 2, 3)
    ]
    right = [(i, (i + 1) % ring) for i in range(ring)]
    left = [(i, (i - 1) % ring) for i in range(ring)]
    other = [(0, 1), (1, 0)]

    def take(steps, total, weight, gain, relative, with_squares):
        index = []
        for i in steps:
            back, ahead = (me_z - i) % ring, (me_z + i) % ring
            mine, others = me_c * ring, (1 - me_c) * ring
            index += [mine + back, others + back, mine + ahead, others + ahead]
        at = [(me_y - p // 4) % 4 * 4 + p % 4 for p in index] if relative else index
        blocks = [v for i in steps for v in held[i]]
        return gather_steps(jnp.stack(at + index), blocks, weight, gain, total, with_squares)

    def score_steps(steps, total):
        return take(steps, total, score_b, gains[0], False, True)

    top, low = packed[:half], packed[half:]
    held = []
    total = None
    for i in range(ring):
        if i == 4:
            score_w, _ = lax.optimization_barrier((score_b, (top, low)))
            score_b = jnp.where(at_home(), score_weight[0], score_w).reshape(parts, feats, hid)
        if i == 5:
            total = score_steps((0, 1, 2, 3), None)
            total, (top, low) = lax.optimization_barrier((total, (top, low)))
        if i == 6:
            total = score_steps((4, 5), total)
            total, quarters, (top, low) = lax.optimization_barrier((total, quarters, (top, low)))
        if i >= 1:
            held[i - 1], (top, low) = lax.optimization_barrier((held[i - 1], (top, low)))
        low_o = lax.ppermute(low, "c", other)
        if i == 0:
            low_o, top = lax.optimization_barrier((low_o, top))
        top_o = lax.ppermute(top, "c", other)
        if i == 0:
            top_o, top = lax.optimization_barrier((top_o, top))
        held.append((top, top_o, low, low_o))
        if i < ring - 1:
            top = lax.ppermute(top, "z", right)
            low = lax.ppermute(low, "z", left)
    total = score_steps((6,), total)
    total = score_steps((7,), total)
    total = total.reshape(slots, hid + 128)
    scale = lax.rsqrt(jnp.sum(total[:, hid:], axis=1) / width + epsilon)
    score_pre = total[:, :hid] * scale[:, None]
    part_score = lax.dot_general(
        heads[:2], jax.nn.silu(score_pre), (((1,), (1,)), ((), ())), precision=lax.Precision.HIGHEST
    )
    actor_b = jnp.concatenate(quarters, axis=0).reshape(parts, feats, hid)
    actor_b, part_score = lax.optimization_barrier((actor_b, part_score))
    totals = jnp.sum(spread(part_score, SLICE), axis=0)
    actor_sum = take((0, 1, 2, 3), None, actor_b, gains[1], True, False)
    actor_sum, totals = lax.optimization_barrier((actor_sum, totals))
    actor_sum = take((4, 5, 6, 7), actor_sum, actor_b, gains[1], True, False)
    actor_pre = actor_sum.reshape(slots, hid) * scale[:, None]
    part_shift = lax.dot_general(
        heads[2:], jax.nn.silu(actor_pre), (((1,), (1,)), ((), ())), precision=lax.Precision.HIGHEST
    )
    shift = jnp.sum(spread(part_shift, SLICE), axis=0)[0]
    code_row = jnp.concatenate([code, jnp.zeros((slots - toks,), jnp.float32)])
    seen = spread(jnp.concatenate([totals, code_row[None]], axis=0), MEMBER)
    scores = seen[:, :2]
    codes = seen[:, 2, :toks].astype(jnp.int32)
    packed_scores = lax.dynamic_index_in_dim(scores, section, 0, keepdims=False)

    every_slot = codes // 2
    every_target = every_slot // cap
    every_place = every_slot % cap
    final = (codes % 2) == 1
    at_place = (every_place[:, :, None] == jnp.arange(cap, dtype=jnp.int32)).astype(jnp.float32)
    at_target = (every_target[:, :, None] == jnp.arange(parts, dtype=jnp.int32)).astype(jnp.float32)
    table = scores.reshape(parts, 2, parts, cap)
    found = jnp.einsum("stj,mksj->kstm", at_place, table, precision=lax.Precision.HIGHEST)
    found = jnp.sum(found * at_target[None], axis=3)
    values, rewards = found[0], found[1]
    raw = jnp.where(final, rewards, shifted(values, 1)) - values
    weight = jnp.where(final, 0.0, trace_decay)
    step = 1
    while step < 128:
        raw = raw + weight * shifted(raw, step)
        weight = weight * shifted(weight, step)
        step *= 2
    total_tokens = raw.size
    center = jnp.sum(raw) / total_tokens
    spread_sq = jnp.sum(raw * raw) / total_tokens - center * center
    every_adv = (raw - center) * lax.rsqrt(spread_sq + epsilon)
    advantages = lax.dynamic_index_in_dim(every_adv, section, 0, keepdims=False)
    mine = jnp.where(every_target == member, every_adv, 0.0)
    adv_slot = jnp.sum(mine[:, :, None] * at_place, axis=1).reshape(slots)

    ratios = jnp.exp(shift)
    slope = penalty * (ratios - 1.0) - ratios * adv_slot
    sig = jax.nn.sigmoid(actor_pre)
    silu_slope = sig * (1.0 + actor_pre * (1.0 - sig))
    grad_pre = ((slope * scale)[:, None] * heads[2][None, :] * silu_slope).astype(jnp.bfloat16)

    halves, to = [], []
    for core, first in ((me_c, 0), (1 - me_c, 1)):
        for i in range(ring):
            halves += [held[i][first], held[(ring - i) % ring][2 + first]]
            to.append(core * ring + (me_z - i) % ring)
    terms = gradient_terms(jnp.stack(to), grad_pre.T, halves)
    arrived = lax.all_to_all(terms, MEMBER, split_axis=0, concat_axis=0, tiled=True)
    grad = flip(jnp.sum(arrived.astype(jnp.float32), axis=0))
    gain = lax.dynamic_slice_in_dim(actor_gain, section * feats, feats)
    actor_grad = grad.T * gain[:, None]
    return (packed_scores, advantages, actor_grad)


def solution(mesh):
    fine = Mesh(mesh.devices.reshape(4, 2, 2, 2, 8), ("y", "l", "c", "h", "z"))
    tensor = ("h", "z")
    in_specs = (
        P(SECTION, tensor),
        P(SECTION, None),
        P(SECTION, None),
        P(SECTION, None),
        P(SECTION, None, tensor),
        P(SECTION, tensor, None),
        P(),
        P(None, tensor),
        P(tensor),
    )
    out_specs = (P(None, SECTION), P(SECTION), P(SECTION, tensor))
    return jax.shard_map(body, mesh=fine, in_specs=in_specs, out_specs=out_specs, check_vma=False)
```

```python
import jax
import jax.numpy as jnp
from jax import lax
from jax.experimental import pallas as pl
from jax.experimental.pallas import tpu as pltpu
from jax.sharding import Mesh, PartitionSpec as P

epsilon = 1e-05
trace_decay = 0.95
penalty = 0.1

SECTION = ("y", "l", "c")
MEMBER = ("y", "l", "h")
SLICE = ("c", "z")


def at_home():
    return lax.axis_index("c") == lax.axis_index("h")


def flip(v):
    got = lax.ppermute(v, ("c", "h"), [(1, 2), (2, 1)])
    return jnp.where(at_home(), v, got)


def flip_far(v):
    return lax.ppermute(v, ("c", "h"), [(1, 2), (2, 1)])


def near_only(v):
    pairs = [(l * 4 + a, (1 - l) * 4 + b) for l in range(2) for a, b in ((1, 2), (2, 1))]
    return lax.ppermute(v, ("l", "c", "h"), pairs)


def gather_steps(place, blocks, weight, gain, total, with_squares):
    rows, feats = blocks[0].shape
    hid = weight.shape[2]
    cols = hid + (128 if with_squares else 0)
    tile = rows // 2
    count = len(blocks)

    def kernel(place_ref, *refs):
        xs, ws, gs = refs[:count], refs[count : 2 * count], refs[2 * count : 3 * count]
        out_ref = refs[-1]
        for side in range(2):
            acc = None if total is None else refs[3 * count][side, :, :hid]
            squares = None
            if with_squares:
                squares = (
                    jnp.zeros((tile, 128), jnp.float32)
                    if total is None
                    else refs[3 * count][side, :, hid:]
                )
            for k in range(count):
                if k % 4 // 2 != side:
                    continue
                wide = xs[k][...].astype(jnp.float32)
                scaled = (wide * gs[k][0]).astype(jnp.bfloat16)
                term = jnp.dot(scaled, ws[k][0], preferred_element_type=jnp.float32)
                acc = term if acc is None else acc + term
                if with_squares:
                    square = wide * wide
                    for j in range(feats // 128):
                        squares = squares + square[:, j * 128 : (j + 1) * 128]
            out_ref[side, :, :hid] = acc
            if with_squares:
                out_ref[side, :, hid:] = squares

    def pick(shape, at):
        return pl.BlockSpec(shape, lambda r, p: (p[at], 0, 0))

    x_spec = pl.BlockSpec((tile, feats), lambda r, p: (r, 0))
    acc_spec = pl.BlockSpec((2, tile, cols), lambda r, p: (0, r, 0))
    in_specs = [x_spec] * count
    in_specs += [pick((1, feats, hid), at) for at in range(count)]
    in_specs += [pick((1, 1, feats), count + at) for at in range(count)]
    operands = [place, *blocks] + [weight] * count + [gain] * count
    aliases = {}
    if total is not None:
        aliases = {len(operands): 0}
        operands.append(total)
        in_specs.append(acc_spec)
    return pl.pallas_call(
        kernel,
        out_shape=jax.ShapeDtypeStruct((2, rows, cols), jnp.float32),
        grid_spec=pltpu.PrefetchScalarGridSpec(
            num_scalar_prefetch=1, grid=(2,), in_specs=in_specs, out_specs=acc_spec
        ),
        input_output_aliases=aliases,
        compiler_params=pltpu.CompilerParams(vmem_limit_bytes=60 << 20),
        cost_estimate=pl.CostEstimate(
            flops=2 * count * rows * feats * hid,
            bytes_accessed=(3 * count // 2 + 5) << 19,
            transcendentals=0,
        ),
    )(*operands)


def gradient_terms(place, slope_t, halves):
    count = len(halves) // 2
    hid = slope_t.shape[0]
    rows, feats = halves[0].shape

    def kernel(place_ref, slope_ref, *refs):
        blocks = refs[: 2 * count]
        out_ref, held, made, sems, out_sems = refs[2 * count :]

        def fetch(k, side):
            return pltpu.make_async_copy(
                blocks[2 * k + side], held.at[k, pl.ds(side * rows, rows)], sems.at[k, side]
            )

        def put(k):
            return pltpu.make_async_copy(made.at[k], out_ref.at[place_ref[k]], out_sems.at[k])

        for k in range(count):
            for side in range(2):
                fetch(k, side).start()
        for k in range(count):
            for side in range(2):
                fetch(k, side).wait()
            made[k] = jnp.dot(
                slope_ref[...], held[k], preferred_element_type=jnp.float32
            ).astype(jnp.bfloat16)
            put(k).start()
        for k in range(count):
            put(k).wait()

    anywhere = pl.BlockSpec(memory_space=pl.ANY)
    return pl.pallas_call(
        kernel,
        out_shape=jax.ShapeDtypeStruct((count, hid, feats), jnp.bfloat16),
        grid_spec=pltpu.PrefetchScalarGridSpec(
            num_scalar_prefetch=1,
            grid=(1,),
            in_specs=[pl.BlockSpec((hid, 2 * rows), lambda r, p: (0, 0))] + [anywhere] * (2 * count),
            out_specs=anywhere,
            scratch_shapes=[
                pltpu.VMEM((count, 2 * rows, feats), jnp.bfloat16),
                pltpu.VMEM((count, hid, feats), jnp.bfloat16),
                pltpu.SemaphoreType.DMA((count, 2)),
                pltpu.SemaphoreType.DMA((count,)),
            ],
        ),
        compiler_params=pltpu.CompilerParams(vmem_limit_bytes=60 << 20),
        cost_estimate=pl.CostEstimate(
            flops=2 * count * 2 * rows * feats * hid, bytes_accessed=21 << 20, transcendentals=0
        ),
    )(place, slope_t, *halves)


def spread(v, axes):
    return lax.all_to_all(
        jnp.broadcast_to(v[None], (16,) + v.shape), axes, split_axis=0, concat_axis=0, tiled=True
    )


def number(axes):
    return lax.axis_index(axes)


def shifted(v, k):
    return jnp.concatenate([v[:, k:], jnp.zeros_like(v[:, :k])], axis=1)


def body(
    states,
    lengths,
    routes,
    score_gain,
    score_weight,
    score_heads,
    actor_gain,
    actor_weight,
    actor_heads,
):
    toks = states.shape[0]
    feats = states.shape[1]
    width = actor_gain.shape[0]
    hid = actor_heads.shape[0]
    parts = 16
    cap = 2 * toks // parts
    slots = parts * cap
    half = slots // 2
    ring = 8
    me_z = number("z")
    me_c = number("c")
    section = number(SECTION)
    member = number(MEMBER)

    meta = flip(jnp.concatenate([routes[:, 0], lengths[0]]))
    moved = flip(states)
    target = meta[:toks]
    spans = meta[toks:]
    pos = jnp.arange(toks, dtype=jnp.int32)
    onehot = target[:, None] == jnp.arange(parts, dtype=jnp.int32)[None, :]
    earlier = (pos[:, None] > pos[None, :]).astype(jnp.bfloat16)
    before = jnp.dot(earlier, onehot.astype(jnp.bfloat16), preferred_element_type=jnp.float32)
    placed = jnp.sum(jnp.where(onehot, before, 0.0), axis=1).astype(jnp.int32)
    slot = target * cap + placed
    order = jnp.arange(spans.shape[0], dtype=jnp.int32)
    ends = jnp.sum(jnp.where(order[:, None] >= order[None, :], spans[None, :], 0), axis=1) - 1
    last = jnp.any(pos[:, None] == ends[None, :], axis=1)
    code = (slot * 2 + last.astype(jnp.int32)).astype(jnp.float32)

    (own_heads, own_shift, own_gain), meta = lax.optimization_barrier(
        ((score_heads, actor_heads, score_gain), meta)
    )
    small = flip(
        jnp.concatenate([own_heads[0].T.reshape(-1), own_shift, own_gain[0]], axis=0)
    )

    dispatch = (jnp.arange(slots, dtype=jnp.int32)[:, None] == slot[None, :]).astype(jnp.bfloat16)
    outbox = jnp.dot(dispatch, moved, preferred_element_type=jnp.float32).astype(jnp.bfloat16)
    packed = lax.all_to_all(
        outbox.reshape(parts, cap, feats), MEMBER, split_axis=0, concat_axis=0, tiled=True
    ).reshape(slots, feats)

    (late_w, small), packed = lax.optimization_barrier(((score_weight[0], small), packed))
    score_b = flip_far(late_w)
    heads = small[: 3 * hid].reshape(3, hid)
    gains = (small[3 * hid :].reshape(parts, 1, feats), actor_gain.reshape(parts, 1, feats))

    right = [(i, (i + 1) % ring) for i in range(ring)]
    left = [(i, (i - 1) % ring) for i in range(ring)]
    other = [(0, 1), (1, 0)]

    def take(steps, total, weight, gain, with_squares):
        index = []
        for i in steps:
            back, ahead = (me_z - i) % ring, (me_z + i) % ring
            mine, others = me_c * ring, (1 - me_c) * ring
            index += [mine + back, others + back, mine + ahead, others + ahead]
        blocks = [v for i in steps for v in held[i]]
        return gather_steps(jnp.stack(index + index), blocks, weight, gain, total, with_squares)

    def score_steps(steps, total):
        return take(steps, total, score_b, gains[0], True)

    top, low = packed[:half], packed[half:]
    held = []
    total = None
    for i in range(ring):
        if i == 4:
            score_w, _, near_w = lax.optimization_barrier((score_b, (top, low), actor_weight))
            actor_w = near_only(near_w)
            score_b = jnp.where(at_home(), score_weight[0], score_w).reshape(parts, feats, hid)
        if i == 5:
            total = score_steps((0, 1, 2, 3), None)
            total, (top, low) = lax.optimization_barrier((total, (top, low)))
        if i == 6:
            total = score_steps((4, 5), total)
            total, (top, low) = lax.optimization_barrier((total, (top, low)))
        if i >= 1:
            held[i - 1], (top, low) = lax.optimization_barrier((held[i - 1], (top, low)))
        low_o = lax.ppermute(low, "c", other)
        if i == 0:
            low_o, top = lax.optimization_barrier((low_o, top))
        top_o = lax.ppermute(top, "c", other)
        if i == 0:
            top_o, top = lax.optimization_barrier((top_o, top))
        held.append((top, top_o, low, low_o))
        if i < ring - 1:
            top = lax.ppermute(top, "z", right)
            low = lax.ppermute(low, "z", left)
    total = score_steps((6,), total)
    total = score_steps((7,), total)
    total = total.reshape(slots, hid + 128)
    scale = lax.rsqrt(jnp.sum(total[:, hid:], axis=1) / width + epsilon)
    score_pre = total[:, :hid] * scale[:, None]
    part_score = lax.dot_general(
        heads[:2], jax.nn.silu(score_pre), (((1,), (1,)), ((), ())), precision=lax.Precision.HIGHEST
    )
    actor_w, part_score = lax.optimization_barrier((actor_w, part_score))
    actor_b = jnp.where(at_home(), actor_weight, actor_w).reshape(parts, feats, hid)
    totals = jnp.sum(spread(part_score, SLICE), axis=0)
    actor_sum = take((0, 1, 2, 3), None, actor_b, gains[1], False)
    actor_sum, totals = lax.optimization_barrier((actor_sum, totals))
    actor_sum = take((4, 5, 6, 7), actor_sum, actor_b, gains[1], False)
    actor_pre = actor_sum.reshape(slots, hid) * scale[:, None]
    part_shift = lax.dot_general(
        heads[2:], jax.nn.silu(actor_pre), (((1,), (1,)), ((), ())), precision=lax.Precision.HIGHEST
    )
    code_row = jnp.concatenate([code, jnp.zeros((slots - toks,), jnp.float32)])
    seen = spread(jnp.concatenate([totals, code_row[None]], axis=0), MEMBER)
    seen, part_shift = lax.optimization_barrier((seen, part_shift))
    shift = jnp.sum(spread(part_shift, SLICE), axis=0)[0]
    scores = seen[:, :2]
    codes = seen[:, 2, :toks].astype(jnp.int32)
    packed_scores = lax.dynamic_index_in_dim(scores, section, 0, keepdims=False)

    every_slot = codes // 2
    every_target = every_slot // cap
    every_place = every_slot % cap
    final = (codes % 2) == 1
    at_place = (every_place[:, :, None] == jnp.arange(cap, dtype=jnp.int32)).astype(jnp.float32)
    at_target = (every_target[:, :, None] == jnp.arange(parts, dtype=jnp.int32)).astype(jnp.float32)
    table = scores.reshape(parts, 2, parts, cap)
    found = jnp.einsum("stj,mksj->kstm", at_place, table, precision=lax.Precision.HIGHEST)
    found = jnp.sum(found * at_target[None], axis=3)
    values, rewards = found[0], found[1]
    raw = jnp.where(final, rewards, shifted(values, 1)) - values
    weight = jnp.where(final, 0.0, trace_decay)
    step = 1
    while step < 128:
        raw = raw + weight * shifted(raw, step)
        weight = weight * shifted(weight, step)
        step *= 2
    total_tokens = raw.size
    center = jnp.sum(raw) / total_tokens
    spread_sq = jnp.sum(raw * raw) / total_tokens - center * center
    every_adv = (raw - center) * lax.rsqrt(spread_sq + epsilon)
    advantages = lax.dynamic_index_in_dim(every_adv, section, 0, keepdims=False)
    mine = jnp.where(every_target == member, every_adv, 0.0)
    adv_slot = jnp.sum(mine[:, :, None] * at_place, axis=1).reshape(slots)

    ratios = jnp.exp(shift)
    slope = penalty * (ratios - 1.0) - ratios * adv_slot
    sig = jax.nn.sigmoid(actor_pre)
    silu_slope = sig * (1.0 + actor_pre * (1.0 - sig))
    grad_pre = ((slope * scale)[:, None] * heads[2][None, :] * silu_slope).astype(jnp.bfloat16)

    halves, to = [], []
    for core, first in ((me_c, 0), (1 - me_c, 1)):
        for i in range(ring):
            halves += [held[i][first], held[(ring - i) % ring][2 + first]]
            to.append(core * ring + (me_z - i) % ring)
    terms = gradient_terms(jnp.stack(to), grad_pre.T, halves)
    arrived = lax.all_to_all(terms, MEMBER, split_axis=0, concat_axis=0, tiled=True)
    grad = flip(jnp.sum(arrived.astype(jnp.float32), axis=0))
    gain = lax.dynamic_slice_in_dim(actor_gain, section * feats, feats)
    actor_grad = grad.T * gain[:, None]
    return (packed_scores, advantages, actor_grad)


def solution(mesh):
    fine = Mesh(mesh.devices.reshape(4, 2, 2, 2, 8), ("y", "l", "c", "h", "z"))
    tensor = ("h", "z")
    in_specs = (
        P(SECTION, tensor),
        P(SECTION, None),
        P(SECTION, None),
        P(SECTION, None),
        P(SECTION, None, tensor),
        P(SECTION, tensor, None),
        P(),
        P(None, tensor),
        P(tensor),
    )
    out_specs = (P(None, SECTION), P(SECTION), P(SECTION, tensor))
    return jax.shard_map(body, mesh=fine, in_specs=in_specs, out_specs=out_specs, check_vma=False)
```

```python
import jax
import jax.numpy as jnp
from jax import lax
from jax.experimental import pallas as pl
from jax.experimental.pallas import tpu as pltpu
from jax.sharding import Mesh, PartitionSpec as P

epsilon = 1e-05
trace_decay = 0.95
penalty = 0.1

SECTION = ("y", "l", "c")
MEMBER = ("y", "l", "h")
SLICE = ("c", "z")


def at_home():
    return lax.axis_index("c") == lax.axis_index("h")


def flip(v):
    got = lax.ppermute(v, ("c", "h"), [(1, 2), (2, 1)])
    return jnp.where(at_home(), v, got)


def flip_far(v):
    return lax.ppermute(v, ("c", "h"), [(1, 2), (2, 1)])


def near_only(v):
    pairs = [(l * 4 + a, (1 - l) * 4 + b) for l in range(2) for a, b in ((1, 2), (2, 1))]
    return lax.ppermute(v, ("l", "c", "h"), pairs)


def gather_steps(place, blocks, weight, gain, total, with_squares):
    rows, feats = blocks[0].shape
    hid = weight.shape[2]
    cols = hid + (128 if with_squares else 0)
    tile = rows // 2
    count = len(blocks)

    def kernel(place_ref, *refs):
        xs, ws, gs = refs[:count], refs[count : 2 * count], refs[2 * count : 3 * count]
        out_ref = refs[-1]
        for side in range(2):
            acc = None if total is None else refs[3 * count][side, :, :hid]
            squares = None
            if with_squares:
                squares = (
                    jnp.zeros((tile, 128), jnp.float32)
                    if total is None
                    else refs[3 * count][side, :, hid:]
                )
            for k in range(count):
                if k % 4 // 2 != side:
                    continue
                wide = xs[k][...].astype(jnp.float32)
                scaled = (wide * gs[k][0]).astype(jnp.bfloat16)
                term = jnp.dot(scaled, ws[k][0], preferred_element_type=jnp.float32)
                acc = term if acc is None else acc + term
                if with_squares:
                    square = wide * wide
                    for j in range(feats // 128):
                        squares = squares + square[:, j * 128 : (j + 1) * 128]
            out_ref[side, :, :hid] = acc
            if with_squares:
                out_ref[side, :, hid:] = squares

    def pick(shape, at):
        return pl.BlockSpec(shape, lambda r, p: (p[at], 0, 0))

    x_spec = pl.BlockSpec((tile, feats), lambda r, p: (r, 0))
    acc_spec = pl.BlockSpec((2, tile, cols), lambda r, p: (0, r, 0))
    in_specs = [x_spec] * count
    in_specs += [pick((1, feats, hid), at) for at in range(count)]
    in_specs += [pick((1, 1, feats), count + at) for at in range(count)]
    operands = [place, *blocks] + [weight] * count + [gain] * count
    aliases = {}
    if total is not None:
        aliases = {len(operands): 0}
        operands.append(total)
        in_specs.append(acc_spec)
    return pl.pallas_call(
        kernel,
        out_shape=jax.ShapeDtypeStruct((2, rows, cols), jnp.float32),
        grid_spec=pltpu.PrefetchScalarGridSpec(
            num_scalar_prefetch=1, grid=(2,), in_specs=in_specs, out_specs=acc_spec
        ),
        input_output_aliases=aliases,
        compiler_params=pltpu.CompilerParams(vmem_limit_bytes=60 << 20),
        cost_estimate=pl.CostEstimate(
            flops=2 * count * rows * feats * hid,
            bytes_accessed=(3 * count // 2 + 5) << 19,
            transcendentals=0,
        ),
    )(*operands)


def gradient_terms(place, slope_t, halves):
    count = len(halves) // 2
    hid = slope_t.shape[0]
    rows, feats = halves[0].shape

    def kernel(place_ref, slope_ref, *refs):
        blocks = refs[: 2 * count]
        out_ref, held, made, sems, out_sems = refs[2 * count :]

        def fetch(k, side):
            return pltpu.make_async_copy(
                blocks[2 * k + side], held.at[k, pl.ds(side * rows, rows)], sems.at[k, side]
            )

        def put(k):
            return pltpu.make_async_copy(made.at[k], out_ref.at[place_ref[k]], out_sems.at[k])

        for k in range(count):
            for side in range(2):
                fetch(k, side).start()
        for k in range(count):
            for side in range(2):
                fetch(k, side).wait()
            made[k] = jnp.dot(
                slope_ref[...], held[k], preferred_element_type=jnp.float32
            ).astype(jnp.bfloat16)
            put(k).start()
        for k in range(count):
            put(k).wait()

    anywhere = pl.BlockSpec(memory_space=pl.ANY)
    return pl.pallas_call(
        kernel,
        out_shape=jax.ShapeDtypeStruct((count, hid, feats), jnp.bfloat16),
        grid_spec=pltpu.PrefetchScalarGridSpec(
            num_scalar_prefetch=1,
            grid=(1,),
            in_specs=[pl.BlockSpec((hid, 2 * rows), lambda r, p: (0, 0))] + [anywhere] * (2 * count),
            out_specs=anywhere,
            scratch_shapes=[
                pltpu.VMEM((count, 2 * rows, feats), jnp.bfloat16),
                pltpu.VMEM((count, hid, feats), jnp.bfloat16),
                pltpu.SemaphoreType.DMA((count, 2)),
                pltpu.SemaphoreType.DMA((count,)),
            ],
        ),
        compiler_params=pltpu.CompilerParams(vmem_limit_bytes=60 << 20),
        cost_estimate=pl.CostEstimate(
            flops=2 * count * 2 * rows * feats * hid, bytes_accessed=21 << 20, transcendentals=0
        ),
    )(place, slope_t, *halves)


def spread(v, axes):
    return lax.all_to_all(
        jnp.broadcast_to(v[None], (16,) + v.shape), axes, split_axis=0, concat_axis=0, tiled=True
    )


def number(axes):
    return lax.axis_index(axes)


def shifted(v, k):
    return jnp.concatenate([v[:, k:], jnp.zeros_like(v[:, :k])], axis=1)


def body(
    states,
    lengths,
    routes,
    score_gain,
    score_weight,
    score_heads,
    actor_gain,
    actor_weight,
    actor_heads,
):
    toks = states.shape[0]
    feats = states.shape[1]
    width = actor_gain.shape[0]
    hid = actor_heads.shape[0]
    parts = 16
    cap = 2 * toks // parts
    slots = parts * cap
    half = slots // 2
    ring = 8
    me_z = number("z")
    me_c = number("c")
    section = number(SECTION)
    member = number(MEMBER)

    meta = flip(jnp.concatenate([routes[:, 0], lengths[0]]))
    moved = flip(states)
    target = meta[:toks]
    spans = meta[toks:]
    pos = jnp.arange(toks, dtype=jnp.int32)
    onehot = target[:, None] == jnp.arange(parts, dtype=jnp.int32)[None, :]
    earlier = (pos[:, None] > pos[None, :]).astype(jnp.bfloat16)
    before = jnp.dot(earlier, onehot.astype(jnp.bfloat16), preferred_element_type=jnp.float32)
    placed = jnp.sum(jnp.where(onehot, before, 0.0), axis=1).astype(jnp.int32)
    slot = target * cap + placed
    order = jnp.arange(spans.shape[0], dtype=jnp.int32)
    ends = jnp.sum(jnp.where(order[:, None] >= order[None, :], spans[None, :], 0), axis=1) - 1
    last = jnp.any(pos[:, None] == ends[None, :], axis=1)
    code = (slot * 2 + last.astype(jnp.int32)).astype(jnp.float32)

    (own_heads, own_shift, own_gain), meta = lax.optimization_barrier(
        ((score_heads, actor_heads, score_gain), meta)
    )
    own_small = jnp.concatenate([own_heads[0].T.reshape(-1), own_shift, own_gain[0]], axis=0)
    got_small = flip_far(own_small)

    dispatch = (jnp.arange(slots, dtype=jnp.int32)[:, None] == slot[None, :]).astype(jnp.bfloat16)
    outbox = jnp.dot(dispatch, moved, preferred_element_type=jnp.float32).astype(jnp.bfloat16)
    packed = lax.all_to_all(
        outbox.reshape(parts, cap, feats), MEMBER, split_axis=0, concat_axis=0, tiled=True
    ).reshape(slots, feats)

    late_w, packed = lax.optimization_barrier((score_weight[0], packed))
    score_b = flip_far(late_w)

    right = [(i, (i + 1) % ring) for i in range(ring)]
    left = [(i, (i - 1) % ring) for i in range(ring)]
    other = [(0, 1), (1, 0)]

    def take(steps, total, weight, gain, with_squares):
        index = []
        for i in steps:
            back, ahead = (me_z - i) % ring, (me_z + i) % ring
            mine, others = me_c * ring, (1 - me_c) * ring
            index += [mine + back, others + back, mine + ahead, others + ahead]
        blocks = [v for i in steps for v in held[i]]
        return gather_steps(jnp.stack(index + index), blocks, weight, gain, total, with_squares)

    def score_steps(steps, total):
        return take(steps, total, score_b, gains[0], True)

    top, low = packed[:half], packed[half:]
    held = []
    total = None
    for i in range(ring):
        if i == 4:
            score_w, _, near_w, got_small = lax.optimization_barrier(
                (score_b, (top, low), actor_weight, got_small)
            )
            small = jnp.where(at_home(), own_small, got_small)
            heads = small[: 3 * hid].reshape(3, hid)
            gains = (
                small[3 * hid :].reshape(parts, 1, feats),
                actor_gain.reshape(parts, 1, feats),
            )
            actor_w = near_only(near_w)
            score_b = jnp.where(at_home(), score_weight[0], score_w).reshape(parts, feats, hid)
        if i == 5:
            total = score_steps((0, 1, 2, 3), None)
            total, (top, low) = lax.optimization_barrier((total, (top, low)))
        if i == 6:
            total = score_steps((4, 5), total)
            total, (top, low) = lax.optimization_barrier((total, (top, low)))
        if i >= 1:
            held[i - 1], (top, low) = lax.optimization_barrier((held[i - 1], (top, low)))
        low_o = lax.ppermute(low, "c", other)
        if i == 0:
            low_o, top = lax.optimization_barrier((low_o, top))
        top_o = lax.ppermute(top, "c", other)
        if i == 0:
            top_o, top = lax.optimization_barrier((top_o, top))
        held.append((top, top_o, low, low_o))
        if i < ring - 1:
            top = lax.ppermute(top, "z", right)
            low = lax.ppermute(low, "z", left)
    total = score_steps((6,), total)
    total = score_steps((7,), total)
    total = total.reshape(slots, hid + 128)
    scale = lax.rsqrt(jnp.sum(total[:, hid:], axis=1) / width + epsilon)
    score_pre = total[:, :hid] * scale[:, None]
    part_score = lax.dot_general(
        heads[:2], jax.nn.silu(score_pre), (((1,), (1,)), ((), ())), precision=lax.Precision.HIGHEST
    )
    actor_w, part_score = lax.optimization_barrier((actor_w, part_score))
    actor_b = jnp.where(at_home(), actor_weight, actor_w).reshape(parts, feats, hid)
    totals = jnp.sum(spread(part_score, SLICE), axis=0)
    actor_sum = take((0, 1, 2, 3), None, actor_b, gains[1], False)
    actor_sum, totals = lax.optimization_barrier((actor_sum, totals))
    actor_sum = take((4, 5, 6, 7), actor_sum, actor_b, gains[1], False)
    actor_pre = actor_sum.reshape(slots, hid) * scale[:, None]
    part_shift = lax.dot_general(
        heads[2:], jax.nn.silu(actor_pre), (((1,), (1,)), ((), ())), precision=lax.Precision.HIGHEST
    )
    code_row = jnp.concatenate([code, jnp.zeros((slots - toks,), jnp.float32)])
    seen = spread(jnp.concatenate([totals, code_row[None]], axis=0), MEMBER)
    seen, part_shift = lax.optimization_barrier((seen, part_shift))
    shift = jnp.sum(spread(part_shift, SLICE), axis=0)[0]
    scores = seen[:, :2]
    codes = seen[:, 2, :toks].astype(jnp.int32)
    packed_scores = lax.dynamic_index_in_dim(scores, section, 0, keepdims=False)

    every_slot = codes // 2
    every_target = every_slot // cap
    every_place = every_slot % cap
    final = (codes % 2) == 1
    at_place = (every_place[:, :, None] == jnp.arange(cap, dtype=jnp.int32)).astype(jnp.float32)
    at_target = (every_target[:, :, None] == jnp.arange(parts, dtype=jnp.int32)).astype(jnp.float32)
    table = scores.reshape(parts, 2, parts, cap)
    found = jnp.einsum("stj,mksj->kstm", at_place, table, precision=lax.Precision.HIGHEST)
    found = jnp.sum(found * at_target[None], axis=3)
    values, rewards = found[0], found[1]
    raw = jnp.where(final, rewards, shifted(values, 1)) - values
    weight = jnp.where(final, 0.0, trace_decay)
    step = 1
    while step < 128:
        raw = raw + weight * shifted(raw, step)
        weight = weight * shifted(weight, step)
        step *= 2
    total_tokens = raw.size
    center = jnp.sum(raw) / total_tokens
    spread_sq = jnp.sum(raw * raw) / total_tokens - center * center
    every_adv = (raw - center) * lax.rsqrt(spread_sq + epsilon)
    advantages = lax.dynamic_index_in_dim(every_adv, section, 0, keepdims=False)
    mine = jnp.where(every_target == member, every_adv, 0.0)
    adv_slot = jnp.sum(mine[:, :, None] * at_place, axis=1).reshape(slots)

    ratios = jnp.exp(shift)
    slope = penalty * (ratios - 1.0) - ratios * adv_slot
    sig = jax.nn.sigmoid(actor_pre)
    silu_slope = sig * (1.0 + actor_pre * (1.0 - sig))
    grad_pre = ((slope * scale)[:, None] * heads[2][None, :] * silu_slope).astype(jnp.bfloat16)

    halves, to = [], []
    for core, first in ((me_c, 0), (1 - me_c, 1)):
        for i in range(ring):
            halves += [held[i][first], held[(ring - i) % ring][2 + first]]
            to.append(core * ring + (me_z - i) % ring)
    terms = gradient_terms(jnp.stack(to), grad_pre.T, halves)
    arrived = lax.all_to_all(terms, MEMBER, split_axis=0, concat_axis=0, tiled=True)
    grad = flip(jnp.sum(arrived.astype(jnp.float32), axis=0))
    gain = lax.dynamic_slice_in_dim(actor_gain, section * feats, feats)
    actor_grad = grad.T * gain[:, None]
    return (packed_scores, advantages, actor_grad)


def solution(mesh):
    fine = Mesh(mesh.devices.reshape(4, 2, 2, 2, 8), ("y", "l", "c", "h", "z"))
    tensor = ("h", "z")
    in_specs = (
        P(SECTION, tensor),
        P(SECTION, None),
        P(SECTION, None),
        P(SECTION, None),
        P(SECTION, None, tensor),
        P(SECTION, tensor, None),
        P(),
        P(None, tensor),
        P(tensor),
    )
    out_specs = (P(None, SECTION), P(SECTION), P(SECTION, tensor))
    return jax.shard_map(body, mesh=fine, in_specs=in_specs, out_specs=out_specs, check_vma=False)
```

```python
import jax
import jax.numpy as jnp
from jax import lax
from jax.experimental import pallas as pl
from jax.experimental.pallas import tpu as pltpu
from jax.sharding import Mesh, PartitionSpec as P

epsilon = 1e-05
trace_decay = 0.95
penalty = 0.1

SECTION = ("y", "l", "c")
MEMBER = ("y", "l", "h")
SLICE = ("c", "z")


def at_home():
    return lax.axis_index("c") == lax.axis_index("h")


def flip(v):
    got = lax.ppermute(v, ("c", "h"), [(1, 2), (2, 1)])
    return jnp.where(at_home(), v, got)


def flip_far(v):
    return lax.ppermute(v, ("c", "h"), [(1, 2), (2, 1)])


def near_only(v):
    pairs = [(l * 4 + a, (1 - l) * 4 + b) for l in range(2) for a, b in ((1, 2), (2, 1))]
    return lax.ppermute(v, ("l", "c", "h"), pairs)


def gather_steps(place, blocks, weight, gain, total, with_squares):
    rows, feats = blocks[0].shape
    hid = weight.shape[2]
    cols = hid + (128 if with_squares else 0)
    tile = rows // 2
    count = len(blocks)

    def kernel(place_ref, *refs):
        xs, ws, gs = refs[:count], refs[count : 2 * count], refs[2 * count : 3 * count]
        out_ref = refs[-1]
        for side in range(2):
            acc = None if total is None else refs[3 * count][side, :, :hid]
            squares = None
            if with_squares:
                squares = (
                    jnp.zeros((tile, 128), jnp.float32)
                    if total is None
                    else refs[3 * count][side, :, hid:]
                )
            for k in range(count):
                if k % 4 // 2 != side:
                    continue
                wide = xs[k][...].astype(jnp.float32)
                scaled = (wide * gs[k][0]).astype(jnp.bfloat16)
                term = jnp.dot(scaled, ws[k][0], preferred_element_type=jnp.float32)
                acc = term if acc is None else acc + term
                if with_squares:
                    square = wide * wide
                    for j in range(feats // 128):
                        squares = squares + square[:, j * 128 : (j + 1) * 128]
            out_ref[side, :, :hid] = acc
            if with_squares:
                out_ref[side, :, hid:] = squares

    def pick(shape, at):
        return pl.BlockSpec(shape, lambda r, p: (p[at], 0, 0))

    x_spec = pl.BlockSpec((tile, feats), lambda r, p: (r, 0))
    acc_spec = pl.BlockSpec((2, tile, cols), lambda r, p: (0, r, 0))
    in_specs = [x_spec] * count
    in_specs += [pick((1, feats, hid), at) for at in range(count)]
    in_specs += [pick((1, 1, feats), count + at) for at in range(count)]
    operands = [place, *blocks] + [weight] * count + [gain] * count
    aliases = {}
    if total is not None:
        aliases = {len(operands): 0}
        operands.append(total)
        in_specs.append(acc_spec)
    return pl.pallas_call(
        kernel,
        out_shape=jax.ShapeDtypeStruct((2, rows, cols), jnp.float32),
        grid_spec=pltpu.PrefetchScalarGridSpec(
            num_scalar_prefetch=1, grid=(2,), in_specs=in_specs, out_specs=acc_spec
        ),
        input_output_aliases=aliases,
        compiler_params=pltpu.CompilerParams(vmem_limit_bytes=60 << 20),
        cost_estimate=pl.CostEstimate(
            flops=2 * count * rows * feats * hid,
            bytes_accessed=(3 * count // 2 + 5) << 19,
            transcendentals=0,
        ),
    )(*operands)


def gradient_terms(place, slope_t, halves):
    count = len(halves) // 2
    hid = slope_t.shape[0]
    rows, feats = halves[0].shape

    def kernel(place_ref, slope_ref, *refs):
        blocks = refs[: 2 * count]
        out_ref, held, made, sems, out_sems = refs[2 * count :]

        def fetch(k, side):
            return pltpu.make_async_copy(
                blocks[2 * k + side], held.at[k, pl.ds(side * rows, rows)], sems.at[k, side]
            )

        def put(k):
            return pltpu.make_async_copy(made.at[k], out_ref.at[place_ref[k]], out_sems.at[k])

        for k in range(count):
            for side in range(2):
                fetch(k, side).start()
        for k in range(count):
            for side in range(2):
                fetch(k, side).wait()
            made[k] = jnp.dot(
                slope_ref[...], held[k], preferred_element_type=jnp.float32
            ).astype(jnp.bfloat16)
            put(k).start()
        for k in range(count):
            put(k).wait()

    anywhere = pl.BlockSpec(memory_space=pl.ANY)
    return pl.pallas_call(
        kernel,
        out_shape=jax.ShapeDtypeStruct((count, hid, feats), jnp.bfloat16),
        grid_spec=pltpu.PrefetchScalarGridSpec(
            num_scalar_prefetch=1,
            grid=(1,),
            in_specs=[pl.BlockSpec((hid, 2 * rows), lambda r, p: (0, 0))] + [anywhere] * (2 * count),
            out_specs=anywhere,
            scratch_shapes=[
                pltpu.VMEM((count, 2 * rows, feats), jnp.bfloat16),
                pltpu.VMEM((count, hid, feats), jnp.bfloat16),
                pltpu.SemaphoreType.DMA((count, 2)),
                pltpu.SemaphoreType.DMA((count,)),
            ],
        ),
        compiler_params=pltpu.CompilerParams(vmem_limit_bytes=60 << 20),
        cost_estimate=pl.CostEstimate(
            flops=2 * count * 2 * rows * feats * hid, bytes_accessed=21 << 20, transcendentals=0
        ),
    )(place, slope_t, *halves)


def spread(v, axes):
    return lax.all_to_all(
        jnp.broadcast_to(v[None], (16,) + v.shape), axes, split_axis=0, concat_axis=0, tiled=True
    )


def number(axes):
    return lax.axis_index(axes)


def shifted(v, k):
    return jnp.concatenate([v[:, k:], jnp.zeros_like(v[:, :k])], axis=1)


def body(
    states,
    lengths,
    routes,
    score_gain,
    score_weight,
    score_heads,
    actor_gain,
    actor_weight,
    actor_heads,
):
    toks = states.shape[0]
    feats = states.shape[1]
    width = actor_gain.shape[0]
    hid = actor_heads.shape[0]
    parts = 16
    cap = 2 * toks // parts
    slots = parts * cap
    half = slots // 2
    ring = 8
    me_z = number("z")
    me_c = number("c")
    section = number(SECTION)
    member = number(MEMBER)

    meta = flip(jnp.concatenate([routes[:, 0], lengths[0]]))
    moved = flip(states)
    target = meta[:toks]
    spans = meta[toks:]
    pos = jnp.arange(toks, dtype=jnp.int32)
    onehot = target[:, None] == jnp.arange(parts, dtype=jnp.int32)[None, :]
    earlier = (pos[:, None] > pos[None, :]).astype(jnp.bfloat16)
    before = jnp.dot(earlier, onehot.astype(jnp.bfloat16), preferred_element_type=jnp.float32)
    placed = jnp.sum(jnp.where(onehot, before, 0.0), axis=1).astype(jnp.int32)
    slot = target * cap + placed
    order = jnp.arange(spans.shape[0], dtype=jnp.int32)
    ends = jnp.sum(jnp.where(order[:, None] >= order[None, :], spans[None, :], 0), axis=1) - 1
    last = jnp.any(pos[:, None] == ends[None, :], axis=1)
    code = (slot * 2 + last.astype(jnp.int32)).astype(jnp.float32)

    (own_heads, own_shift, own_gain), meta = lax.optimization_barrier(
        ((score_heads, actor_heads, score_gain), meta)
    )
    own_small = jnp.concatenate([own_heads[0].T.reshape(-1), own_shift, own_gain[0]], axis=0)
    got_small = flip_far(own_small)

    dispatch = (jnp.arange(slots, dtype=jnp.int32)[:, None] == slot[None, :]).astype(jnp.bfloat16)
    outbox = jnp.dot(dispatch, moved, preferred_element_type=jnp.float32).astype(jnp.bfloat16)
    packed = lax.all_to_all(
        outbox.reshape(parts, cap, feats), MEMBER, split_axis=0, concat_axis=0, tiled=True
    ).reshape(slots, feats)

    late_w, packed = lax.optimization_barrier((score_weight[0], packed))
    score_b = flip_far(late_w)

    right = [(i, (i + 1) % ring) for i in range(ring)]
    left = [(i, (i - 1) % ring) for i in range(ring)]
    other = [(0, 1), (1, 0)]

    def take(steps, total, weight, gain, with_squares):
        index = []
        for i in steps:
            back, ahead = (me_z - i) % ring, (me_z + i) % ring
            mine, others = me_c * ring, (1 - me_c) * ring
            index += [mine + back, others + back, mine + ahead, others + ahead]
        blocks = [v for i in steps for v in held[i]]
        return gather_steps(jnp.stack(index + index), blocks, weight, gain, total, with_squares)

    def score_steps(steps, total):
        return take(steps, total, score_b, gains[0], True)

    top, low = packed[:half], packed[half:]
    held = []
    total = None
    for i in range(ring):
        if i == 4:
            score_w, _, near_w, got_small = lax.optimization_barrier(
                (score_b, (top, low), actor_weight, got_small)
            )
            small = jnp.where(at_home(), own_small, got_small)
            heads = small[: 3 * hid].reshape(3, hid)
            gains = (
                small[3 * hid :].reshape(parts, 1, feats),
                actor_gain.reshape(parts, 1, feats),
            )
            actor_w = near_only(near_w)
            score_b = jnp.where(at_home(), score_weight[0], score_w).reshape(parts, feats, hid)
        if i == 6:
            total = score_steps((0, 1, 2, 3, 4, 5), None)
            total, (top, low) = lax.optimization_barrier((total, (top, low)))
        if i >= 1:
            held[i - 1], (top, low) = lax.optimization_barrier((held[i - 1], (top, low)))
        low_o = lax.ppermute(low, "c", other)
        if i == 0:
            low_o, top = lax.optimization_barrier((low_o, top))
        top_o = lax.ppermute(top, "c", other)
        if i == 0:
            top_o, top = lax.optimization_barrier((top_o, top))
        held.append((top, top_o, low, low_o))
        if i < ring - 1:
            top = lax.ppermute(top, "z", right)
            low = lax.ppermute(low, "z", left)
    total = score_steps((6, 7), total)
    total = total.reshape(slots, hid + 128)
    scale = lax.rsqrt(jnp.sum(total[:, hid:], axis=1) / width + epsilon)
    score_pre = total[:, :hid] * scale[:, None]
    part_score = lax.dot_general(
        heads[:2], jax.nn.silu(score_pre), (((1,), (1,)), ((), ())), precision=lax.Precision.HIGHEST
    )
    actor_w, part_score = lax.optimization_barrier((actor_w, part_score))
    actor_b = jnp.where(at_home(), actor_weight, actor_w).reshape(parts, feats, hid)
    totals = jnp.sum(spread(part_score, SLICE), axis=0)
    actor_sum = take((0, 1, 2, 3), None, actor_b, gains[1], False)
    actor_sum, totals = lax.optimization_barrier((actor_sum, totals))
    actor_sum = take((4, 5, 6, 7), actor_sum, actor_b, gains[1], False)
    actor_pre = actor_sum.reshape(slots, hid) * scale[:, None]
    part_shift = lax.dot_general(
        heads[2:], jax.nn.silu(actor_pre), (((1,), (1,)), ((), ())), precision=lax.Precision.HIGHEST
    )
    code_row = jnp.concatenate([code, jnp.zeros((slots - toks,), jnp.float32)])
    seen = spread(jnp.concatenate([totals, code_row[None]], axis=0), MEMBER)
    seen, part_shift = lax.optimization_barrier((seen, part_shift))
    shift = jnp.sum(spread(part_shift, SLICE), axis=0)[0]
    scores = seen[:, :2]
    codes = seen[:, 2, :toks].astype(jnp.int32)
    packed_scores = lax.dynamic_index_in_dim(scores, section, 0, keepdims=False)

    every_slot = codes // 2
    every_target = every_slot // cap
    every_place = every_slot % cap
    final = (codes % 2) == 1
    at_place = (every_place[:, :, None] == jnp.arange(cap, dtype=jnp.int32)).astype(jnp.float32)
    at_target = (every_target[:, :, None] == jnp.arange(parts, dtype=jnp.int32)).astype(jnp.float32)
    table = scores.reshape(parts, 2, parts, cap)
    found = jnp.einsum("stj,mksj->kstm", at_place, table, precision=lax.Precision.HIGHEST)
    found = jnp.sum(found * at_target[None], axis=3)
    values, rewards = found[0], found[1]
    raw = jnp.where(final, rewards, shifted(values, 1)) - values
    weight = jnp.where(final, 0.0, trace_decay)
    step = 1
    while step < 128:
        raw = raw + weight * shifted(raw, step)
        weight = weight * shifted(weight, step)
        step *= 2
    total_tokens = raw.size
    center = jnp.sum(raw) / total_tokens
    spread_sq = jnp.sum(raw * raw) / total_tokens - center * center
    every_adv = (raw - center) * lax.rsqrt(spread_sq + epsilon)
    advantages = lax.dynamic_index_in_dim(every_adv, section, 0, keepdims=False)
    mine = jnp.where(every_target == member, every_adv, 0.0)
    adv_slot = jnp.sum(mine[:, :, None] * at_place, axis=1).reshape(slots)

    ratios = jnp.exp(shift)
    slope = penalty * (ratios - 1.0) - ratios * adv_slot
    sig = jax.nn.sigmoid(actor_pre)
    silu_slope = sig * (1.0 + actor_pre * (1.0 - sig))
    grad_pre = ((slope * scale)[:, None] * heads[2][None, :] * silu_slope).astype(jnp.bfloat16)

    halves, to = [], []
    for core, first in ((me_c, 0), (1 - me_c, 1)):
        for i in range(ring):
            halves += [held[i][first], held[(ring - i) % ring][2 + first]]
            to.append(core * ring + (me_z - i) % ring)
    terms = gradient_terms(jnp.stack(to), grad_pre.T, halves)
    arrived = lax.all_to_all(terms, MEMBER, split_axis=0, concat_axis=0, tiled=True)
    grad = flip(jnp.sum(arrived.astype(jnp.float32), axis=0))
    gain = lax.dynamic_slice_in_dim(actor_gain, section * feats, feats)
    actor_grad = grad.T * gain[:, None]
    return (packed_scores, advantages, actor_grad)


def solution(mesh):
    fine = Mesh(mesh.devices.reshape(4, 2, 2, 2, 8), ("y", "l", "c", "h", "z"))
    tensor = ("h", "z")
    in_specs = (
        P(SECTION, tensor),
        P(SECTION, None),
        P(SECTION, None),
        P(SECTION, None),
        P(SECTION, None, tensor),
        P(SECTION, tensor, None),
        P(),
        P(None, tensor),
        P(tensor),
    )
    out_specs = (P(None, SECTION), P(SECTION), P(SECTION, tensor))
    return jax.shard_map(body, mesh=fine, in_specs=in_specs, out_specs=out_specs, check_vma=False)
```
